32 devices in a mesh: groups: 2 (over y), dp: 4 (over z), tensor: 4 (over x, core).
Axes of the slice: x: 2, y: 2, z: 4, core: 2. Of those that a mesh axis runs over, the one named last changes fastest.
Arguments:
- hidden: bfloat16 [4096, 7168], P(('groups', 'dp'), 'tensor'), parts along dimension 0, may hold values from -6 to 6
- out_grad: bfloat16 [4096, 4096], P(('groups', 'dp'), 'tensor'), parts along dimension 0, may hold values from -6 to 6
- down_weight: bfloat16 [7168, 4096], P('tensor', 'dp'), may hold values from -0.09375 to 0.09375
- proj_in: bfloat16 [7168, 64], P('tensor'), may hold values from -0.0625 to 0.0625
- proj_out: bfloat16 [4096, 64], replicated, may hold values from -0.09375 to 0.09375
- queries: bfloat16 [4096, 4096], P('dp', 'tensor'), may hold values from -0.005859375 to 0.005859375
Outputs:
- hidden_grad: bfloat16 [4096, 7168], P(('groups', 'dp'), 'tensor'), parts along dimension 0
- scores: float32 [16, 4096], P(('groups', 'dp'), 'tensor'), parts along dimension 0
The draws below stay inside these ranges and needn't reach their ends.
There are 2 independent parts, one for each index of `groups`. The reference program is written for one: setup_inputs(seed, part) draws one part's arguments, and reference() takes and returns one part's arrays. A program takes and returns all parts, laid end to end along the dimension named above; an argument that names none is the same for every part. Nothing has to cross between parts.
All inputs are finite; a program needn't handle non-finite values.
Results may differ from the reference program's by a relative error of at most 0.0028.
Values may be sent and summed in bfloat16 or wider, within the bound.
A program may use at most 128 MiB of HBM per device.

```python
import jax
import jax.numpy as jnp
from jax import lax

D = 4096
FFW = 7168
K = 64
SEQ = 256
NQ = 4096
EXAMPLES = 8
TOKENS = 2048


def levels(rng, shape, cuts, low, top_value):
    loudness, own = 1.0, jax.random.fold_in(rng, 6)
    for dim, parts in cuts:
        draws = jnp.exp(jax.random.uniform(jax.random.fold_in(own, dim), (parts,), jnp.float32, low / len(cuts), top_value / len(cuts)))
        loudness = loudness * jnp.repeat(draws, shape[dim] // parts).reshape([-1 if axis == dim else 1 for axis in range(len(shape))])
    return loudness


def noise(key, dims, deviation, limit, pieces=(), kind=jnp.bfloat16):
    factor_of = levels(key, dims, pieces, -0.22, 0.18) if pieces else 1.0
    entries = jax.random.normal(key, dims, jnp.float32) * deviation * factor_of
    return jnp.minimum(jnp.maximum(entries, -limit), limit).astype(kind)


def setup_inputs(seed: int = 0, part: int = 0) -> dict:
    seeds = jax.random.split(jax.random.key(seed), 7)
    part_splits = jax.random.split(jax.random.fold_in(seeds[6], part), 7)
    hidden = noise(part_splits[0], (TOKENS, FFW), 1.0, 6.0, ((0, 4), (1, 4)))
    out_grad = noise(part_splits[1], (TOKENS, D), 1.0, 6.0, ((0, 4), (1, 4)))
    down_weight = noise(seeds[2], (FFW, D), D ** -0.5, 0.09375, ((0, 4), (1, 4)))
    proj_in = noise(seeds[3], (FFW, K), FFW ** -0.5, 0.0625, ((0, 4),))
    proj_out = noise(seeds[4], (D, K), D ** -0.5, 0.09375)
    queries = noise(seeds[5], (NQ, K * K), (K * K * SEQ) ** -0.5, 0.005859375, ((0, 4), (1, 4)))
    return dict(hidden=hidden, out_grad=out_grad, down_weight=down_weight, proj_in=proj_in, proj_out=proj_out, queries=queries)


def reference(hidden, out_grad, down_weight, proj_in, proj_out, queries):
    grad_wide = out_grad.astype(jnp.float32)
    hidden_grad = jnp.dot(grad_wide, down_weight.astype(jnp.float32).T).astype(jnp.bfloat16)
    left = jnp.dot(hidden, proj_in, preferred_element_type=jnp.float32)
    right = jnp.dot(out_grad, proj_out, preferred_element_type=jnp.float32)
    left = left.reshape(EXAMPLES, SEQ, K)
    right = right.reshape(EXAMPLES, SEQ, K)
    outer = jnp.einsum("esa,esb->eab", left, right, precision=lax.Precision.HIGHEST)
    features = outer.reshape(EXAMPLES, K * K).astype(jnp.bfloat16)
    scores = jnp.dot(features, queries.T, preferred_element_type=jnp.float32)
    return hidden_grad, scores
```

```python
import functools

import jax
import jax.numpy as jnp
from jax import lax
from jax.experimental import pallas as pl
from jax.experimental.pallas import tpu as pltpu
from jax.sharding import PartitionSpec as P

SEQ = 256
NB = 7
VIA = 2
XC = 2
NT = (((1,), (1,)), ((), ()))


def kernel(n, T, hid, og, w, pin, pout, q, hg, sc,
           wg, xg, obuf, lrbuf, gscr, featbuf, sp, spr,
           loc, xz, xo, xs, wsat, wsend, wr, wy, wv, out,
           lrs, fs_, sps, sprr):
    g, p, t = lax.axis_index("groups"), lax.axis_index("dp"), lax.axis_index("tensor")
    tok, dcols = og.shape
    rows, cw = w.shape
    rb = rows // NB
    hf = rb // 2
    xr = tok // XC
    ex = tok // SEQ
    kk = pin.shape[1]
    nh, U = n // 2, T // 2
    nq, fsz = q.shape
    srows = kk // T
    k = p // 2
    hub_of = lambda pair: 2 * pair + 1 - (4 * pair) // n
    hub = hub_of(k)
    sat = 4 * k + 1 - hub
    u, c = t // 2, lax.rem(t, 2)

    def rc(src, dst, ss, rs, **dev):
        return pltpu.make_async_remote_copy(
            src_ref=src, dst_ref=dst, send_sem=ss, recv_sem=rs,
            device_id=dev, device_id_type=pl.DeviceIdType.MESH)

    def cols(i, width):
        return pl.ds(pl.multiple_of(i * width, width), width)

    def half(b, h):
        return pl.ds(pl.multiple_of(b * rb + h * hf, hf), hf)

    def blk(b):
        return pl.ds(pl.multiple_of(b * rb, rb), rb)

    own_x = pltpu.make_async_copy(og, xg.at[pl.ds(0, tok), cols(t, dcols)], loc.at[0])
    own_w = pltpu.make_async_copy(w, wg.at[:, cols(p, cw)], loc.at[1])
    own_x.start()

    @pl.when(p == hub)
    def _():
        own_w.start()

    bar = pltpu.get_barrier_semaphore()

    @pl.loop(1, n * T)
    def _(i):
        other = lax.rem(p * T + t + i, n * T)
        pl.semaphore_signal(bar, inc=1, device_id={"dp": other // T, "tensor": lax.rem(other, T)},
                            device_id_type=pl.DeviceIdType.MESH)

    pl.semaphore_signal(bar, inc=1, device_id={"groups": 1 - g}, device_id_type=pl.DeviceIdType.MESH)
    pl.semaphore_wait(bar, n * T)

    def sat_x(i):
        return rc(og.at[pl.ds(i * xr, xr), :],
                  xg.at[pl.ds(tok + i * xr, xr), cols(t, dcols)],
                  xz.at[0, i], xz.at[1, i], dp=hub)

    def xrow(a, i):
        return pl.ds(a * tok + i * xr, xr)

    def x_far(a, i, d):
        u2 = lax.rem(u + d, U)
        src = og.at[pl.ds(i * xr, xr), :] if a == 0 else xg.at[xrow(a, i), cols(t, dcols)]
        return rc(src, xg.at[xrow(a, i), cols(t, dcols)],
                  xo.at[0, a, i, d], xo.at[1, a, i, d], tensor=2 * u2 + c)

    def x_mate(a, i, d):
        b = 2 * lax.rem(u + U - d, U) + c
        src = og.at[pl.ds(i * xr, xr), :] if a == 0 and d == 0 else xg.at[xrow(a, i), cols(b, dcols)]
        return rc(src, xg.at[xrow(a, i), cols(b, dcols)],
                  xs.at[0, a, i, d], xs.at[1, a, i, d], tensor=2 * u + 1 - c)

    def sat_w(b, o):
        h = g if o == 0 else 1 - g
        return rc(w.at[half(b, h), :], wg.at[half(b, h), cols(sat, cw)],
                  wsend.at[o, b], wsat.at[o, b], dp=hub)

    def hub_w(b, r, s):
        to = hub_of(lax.rem(k + r, nh))
        src = w.at[half(b, g), :] if s == 0 else wg.at[half(b, g), cols(sat, cw)]
        dst = wg.at[half(b, g), cols(p if s == 0 else sat, cw)]
        return rc(src, dst, wr.at[0, s, b, r], wr.at[1, s, b, r], dp=to)

    def y_w(b, r, s):
        k2 = lax.rem(k + nh - r, nh)
        h2 = hub_of(k2)
        at = wg.at[half(b, g), cols(h2 if s == 0 else 4 * k2 + 1 - h2, cw)]
        return rc(at, at, wy.at[0, s, b, r], wy.at[1, s, b, r], groups=1 - g)

    def y_sat(b):
        at = wg.at[half(b, g), cols(sat, cw)]
        return rc(at, at, wv.at[0, b], wv.at[1, b], groups=1 - g)

    def ret(b):
        return rc(obuf.at[:, cols(b, rb)], hg.at[:, cols(b, rb)],
                  out.at[0, b], out.at[1, b], dp=sat)

    def lr_copy(d):
        return rc(lrbuf.at[t], lrbuf.at[t], lrs.at[0, d], lrs.at[1, d],
                  tensor=lax.rem(t + d, T))

    def f_copy(d):
        return rc(featbuf.at[p], featbuf.at[p], fs_.at[0, d], fs_.at[1, d],
                  dp=lax.rem(p + d, n))

    bpt = n // T
    t_to, slot = p // bpt, lax.rem(p, bpt) * T + t

    def s_copy(d):
        p2 = lax.rem(p + d, n)
        return rc(sp.at[p2], spr.at[slot], sps.at[d], sprr.at[slot], dp=p2, tensor=t_to)

    def left_right():
        own_x.wait()
        left = jnp.dot(hid[...], pin[...], preferred_element_type=jnp.float32)
        right = jnp.dot(xg[pl.ds(0, tok), cols(t, dcols)], pout[cols(t, dcols), :],
                        preferred_element_type=jnp.float32)
        lrbuf[t] = jnp.concatenate([left, right], axis=1)
        for d in range(1, T):
            lr_copy(d).start()

    def features():
        for d in range(1, T):
            lr_copy(d).wait_recv()
        R = featbuf.shape[1]
        row = lax.broadcasted_iota(jnp.int32, (R, 2 * kk), 0)
        lane = lax.broadcasted_iota(jnp.int32, (1, 2 * kk), 1)
        for e in range(ex):
            lr = lrbuf[0, pl.ds(e * SEQ, SEQ), :]
            for s in range(1, T):
                lr = lr + lrbuf[s, pl.ds(e * SEQ, SEQ), :]
            right = lr[:, kk:]
            gscr[e] = jnp.dot(lr.T, jnp.concatenate([right, right], axis=1),
                              precision=lax.Precision.HIGHEST,
                              preferred_element_type=jnp.float32)
        mine = [gscr[e, pl.ds(pl.multiple_of(t * srows, srows), srows), :] for e in range(ex)]
        for j in range(srows // 2):
            val = jnp.zeros((R, 2 * kk), jnp.float32)
            for e in range(ex):
                vec = jnp.where(lane < kk, mine[e][2 * j:2 * j + 1], mine[e][2 * j + 1:2 * j + 2])
                val = jnp.where(row == p * ex + e, vec, val)
            featbuf[p, :, pl.ds(j * 2 * kk, 2 * kk)] = val.astype(jnp.bfloat16)
        for d in range(1, n):
            f_copy(d).start()

    def partial_scores():
        for d in range(1, n):
            f_copy(d).wait_recv()
        every = featbuf[0].astype(jnp.float32)
        for s in range(1, n):
            every = every + featbuf[s].astype(jnp.float32)
        s = lax.dot_general(every.astype(jnp.bfloat16), q[...], NT, preferred_element_type=jnp.float32)
        sp[...] = jnp.zeros_like(sp)
        for i in range(n):
            sp[i, 0:ex, :] = s[i * ex:(i + 1) * ex]
        for d in range(1, n):
            s_copy(d).start()

        @pl.when(t_to == t)
        def _():
            spr[slot] = sp[p]

        @pl.when(t_to != t)
        def _():
            s_copy(0).start()

    def finish_scores():
        for i in range(bpt * T):
            me = jnp.logical_and(t * bpt + i // T == p, i % T == t)

            @pl.when(jnp.logical_not(me))
            def _():
                rc(sp.at[0], spr.at[i], sps.at[0], sprr.at[i], dp=p, tensor=t).wait_recv()

        for b in range(bpt):
            tot = spr[b * T, 0:ex, :]
            for s in range(1, T):
                tot = tot + spr[b * T + s, 0:ex, :]
            sc[:, pl.ds(b * nq, nq)] = tot

    @pl.when(p != hub)
    def _():
        for i in range(XC):
            sat_x(i).start()
        order = [(b, 0) for b in range(VIA)]
        for b in range(VIA, NB):
            order.append((b, 0))
            if b > VIA:
                order.append((b - 1, 1))
        order.append((NB - 1, 1))
        for b, o in order:
            sat_w(b, o).start()
        left_right()
        features()
        partial_scores()
        finish_scores()
        for b in range(NB):
            ret(b).wait_recv()
        for i in range(XC):
            sat_x(i).wait_send()
        for b, o in order:
            sat_w(b, o).wait_send()

    @pl.when(p == hub)
    def _():
        for i in range(XC):
            for d in range(1, U):
                x_far(0, i, d).start()
            x_mate(0, i, 0).start()

        @pl.loop(0, NB)
        def _(b):
            @pl.loop(1, nh)
            def _(r):
                hub_w(b, r, 0).start()

        left_right()

        def pass_own(lo, hi):
            @pl.loop(lo, hi)
            def _(b):
                @pl.loop(1, nh)
                def _(r):
                    hub_w(b, r, 0).wait_recv()
                    y_w(b, r, 0).start()

        def pass_x(a, i):
            for d in range(1, U):
                x_far(a, i, d).wait_recv()
                x_mate(a, i, d).start()

        def take_sat(i):
            sat_x(i).wait_recv()
            for d in range(1, U):
                x_far(1, i, d).start()
            x_mate(1, i, 0).start()

        for i in range(XC):
            pass_own(2 * i, 2 * i + 2)
            pass_x(0, i)
            take_sat(i)
        pass_own(2 * XC, NB)
        features()
        pass_x(1, 0)

        @pl.loop(0, NB + 2)
        def _(s):
            @pl.when(s < NB)
            def _():
                sat_w(s, 0).wait_recv()

                @pl.loop(1, nh)
                def _(r):
                    hub_w(s, r, 1).start()

                @pl.when(s < VIA)
                def _():
                    y_sat(s).start()

            @pl.when(jnp.logical_and(s >= 1, s <= NB))
            def _():
                @pl.loop(1, nh)
                def _(r):
                    hub_w(s - 1, r, 1).wait_recv()
                    y_w(s - 1, r, 1).start()

            @pl.when(s == 1)
            def _():
                for i in range(1, XC):
                    pass_x(1, i)
                partial_scores()
                own_w.wait()
                for a in range(2):
                    for i in range(XC):
                        for d in range(U):
                            x_mate(a, i, d).wait_recv()

            @pl.when(s == 3)
            def _():
                finish_scores()

            @pl.when(s >= 2)
            def _():
                b = s - 2

                @pl.loop(1, nh)
                def _(r):
                    for j in range(2):
                        y_w(b, r, j).wait_recv()

                @pl.when(b < VIA)
                def _():
                    y_sat(b).wait_recv()

                @pl.when(b >= VIA)
                def _():
                    sat_w(b, 1).wait_recv()

                @pl.loop(0, tok // SEQ)
                def _(m):
                    at = pl.ds(pl.multiple_of(m * SEQ, SEQ), SEQ)
                    x = xg[pl.ds(pl.multiple_of(tok + m * SEQ, SEQ), SEQ), :]
                    obuf[at, cols(b, rb)] = lax.dot_general(
                        x, wg[blk(b), :], NT, preferred_element_type=jnp.float32
                    ).astype(jnp.bfloat16)

                ret(b).start()

                @pl.loop(0, tok // SEQ)
                def _(m):
                    at = pl.ds(pl.multiple_of(m * SEQ, SEQ), SEQ)
                    hg[at, cols(b, rb)] = lax.dot_general(
                        xg[at, :], wg[blk(b), :], NT, preferred_element_type=jnp.float32
                    ).astype(jnp.bfloat16)

        for a in range(2):
            for i in range(XC):
                for d in range(1, U):
                    x_far(a, i, d).wait_send()
                for d in range(U):
                    x_mate(a, i, d).wait_send()

        @pl.loop(0, NB)
        def _(b):
            @pl.loop(1, nh)
            def _(r):
                for s in range(2):
                    hub_w(b, r, s).wait_send()
                    y_w(b, r, s).wait_send()

            @pl.when(b < VIA)
            def _():
                y_sat(b).wait_send()

            ret(b).wait_send()

    for d in range(1, T):
        lr_copy(d).wait_send()
    for d in range(1, n):
        f_copy(d).wait_send()
        s_copy(d).wait_send()

    @pl.when(t_to != t)
    def _():
        s_copy(0).wait_send()


def local(n, T, hidden, out_grad, down_weight, proj_in, proj_out, queries):
    tok, dcols = out_grad.shape
    rows, cw = down_weight.shape
    kk = proj_in.shape[1]
    ex = tok // SEQ
    nq, fsz = queries.shape
    R = -(-n * ex // 16) * 16
    nh, U = n // 2, T // 2
    bf, f32 = jnp.bfloat16, jnp.float32
    vm, hb = pl.BlockSpec(memory_space=pltpu.VMEM), pl.BlockSpec(memory_space=pl.ANY)
    dma = pltpu.SemaphoreType.DMA
    return pl.pallas_call(
        functools.partial(kernel, n, T),
        out_shape=(jax.ShapeDtypeStruct((tok, rows), bf),
                   jax.ShapeDtypeStruct((ex, nq * n // T), f32)),
        in_specs=[vm, hb, hb, vm, vm, vm],
        out_specs=(vm, vm),
        scratch_shapes=[
            pltpu.VMEM((rows, cw * n), bf),
            pltpu.VMEM((2 * tok, dcols * T), bf),
            pltpu.VMEM((tok, rows), bf),
            pltpu.VMEM((T, tok, 2 * kk), f32),
            pltpu.VMEM((ex, 2 * kk, 2 * kk), f32),
            pltpu.VMEM((n, R, fsz), bf),
            pltpu.VMEM((n, 8, nq), f32),
            pltpu.VMEM((n // T * T, 8, nq), f32),
            dma((2,)),
            dma((2, XC)),
            dma((2, 2, XC, U)),
            dma((2, 2, XC, U)),
            dma((2, NB)),
            dma((2, NB)),
            dma((2, 2, NB, nh)),
            dma((2, 2, NB, nh)),
            dma((2, NB)),
            dma((2, NB)),
            dma((2, T)),
            dma((2, n)),
            dma((n,)),
            dma((n // T * T,)),
        ],
        compiler_params=pltpu.CompilerParams(
            collective_id=0, has_side_effects=True, vmem_limit_bytes=56 * 2**20),
        cost_estimate=pl.CostEstimate(flops=4 * tok * rows * cw * n, bytes_accessed=2 * rows * cw * n,
                                      transcendentals=0),
    )(hidden, out_grad, down_weight, proj_in, proj_out, queries)


def solution(mesh):
    in_specs = (
        P(("groups", "dp"), "tensor"),
        P(("groups", "dp"), "tensor"),
        P("tensor", "dp"),
        P("tensor", None),
        P(),
        P("dp", "tensor"),
    )
    out_specs = (P(("groups", "dp"), "tensor"), P(("groups", "dp"), "tensor"))
    body = functools.partial(local, mesh.shape["dp"], mesh.shape["tensor"])
    return jax.shard_map(body, mesh=mesh, in_specs=in_specs, out_specs=out_specs, check_vma=False)
```

```python
import functools

import jax
import jax.numpy as jnp
from jax import lax
from jax.experimental import pallas as pl
from jax.experimental.pallas import tpu as pltpu
from jax.sharding import PartitionSpec as P

SEQ = 256
NB = 7
VIA = 2
XC = 4
WIN = 3
NT = (((1,), (1,)), ((), ()))


def kernel(n, T, hid, og, w, pin, pout, q, hg, sc,
           wg, xg, obuf, lrbuf, gscr, featbuf, sp, spr,
           loc, xz, xo, xs, wsat, wsend, wr, wy, wv, out,
           lrs, fs_, sps, sprr):
    g, p, t = lax.axis_index("groups"), lax.axis_index("dp"), lax.axis_index("tensor")
    tok, dcols = og.shape
    rows, cw = w.shape
    rb = rows // NB
    hf = rb // 2
    xr = tok // XC
    ex = tok // SEQ
    kk = pin.shape[0]
    nh, U = n // 2, T // 2
    nq, fsz = q.shape
    srows = kk // T
    k = p // 2
    hub_of = lambda pair: 2 * pair + 1 - (4 * pair) // n
    hub = hub_of(k)
    sat = 4 * k + 1 - hub
    u, c = t // 2, lax.rem(t, 2)

    def rc(src, dst, ss, rs, **dev):
        return pltpu.make_async_remote_copy(
            src_ref=src, dst_ref=dst, send_sem=ss, recv_sem=rs,
            device_id=dev, device_id_type=pl.DeviceIdType.MESH)

    def cols(i, width):
        return pl.ds(pl.multiple_of(i * width, width), width)

    def half(b, h):
        return pl.ds(pl.multiple_of(b * rb + h * hf, hf), hf)

    def blk(b):
        return pl.ds(pl.multiple_of(b * rb, rb), rb)

    own_x = pltpu.make_async_copy(og, xg.at[pl.ds(0, tok), cols(t, dcols)], loc.at[0])
    own_w = pltpu.make_async_copy(w, wg.at[:, cols(p, cw)], loc.at[1])
    own_x.start()

    @pl.when(p == hub)
    def _():
        own_w.start()

    bar = pltpu.get_barrier_semaphore()

    @pl.loop(1, n * T)
    def _(i):
        other = lax.rem(p * T + t + i, n * T)
        pl.semaphore_signal(bar, inc=1, device_id={"dp": other // T, "tensor": lax.rem(other, T)},
                            device_id_type=pl.DeviceIdType.MESH)

    pl.semaphore_signal(bar, inc=1, device_id={"groups": 1 - g}, device_id_type=pl.DeviceIdType.MESH)
    pl.semaphore_wait(bar, n * T)

    def sat_x(i):
        return rc(og.at[pl.ds(i * xr, xr), :],
                  xg.at[pl.ds(tok + i * xr, xr), cols(t, dcols)],
                  xz.at[0, i], xz.at[1, i], dp=hub)

    def xrow(a, i):
        return pl.ds(a * tok + i * xr, xr)

    def x_far(a, i, d):
        u2 = lax.rem(u + d, U)
        src = og.at[pl.ds(i * xr, xr), :] if a == 0 else xg.at[xrow(a, i), cols(t, dcols)]
        return rc(src, xg.at[xrow(a, i), cols(t, dcols)],
                  xo.at[0, a, i, d], xo.at[1, a, i, d], tensor=2 * u2 + c)

    def x_mate(a, i, d):
        b = 2 * lax.rem(u + U - d, U) + c
        src = og.at[pl.ds(i * xr, xr), :] if a == 0 and d == 0 else xg.at[xrow(a, i), cols(b, dcols)]
        return rc(src, xg.at[xrow(a, i), cols(b, dcols)],
                  xs.at[0, a, i, d], xs.at[1, a, i, d], tensor=2 * u + 1 - c)

    def sat_w(b, o):
        h = g if o == 0 else 1 - g
        return rc(w.at[half(b, h), :], wg.at[half(b, h), cols(sat, cw)],
                  wsend.at[o, b], wsat.at[o, b], dp=hub)

    def hub_w(b, r, s):
        to = hub_of(lax.rem(k + r, nh))
        src = w.at[half(b, g), :] if s == 0 else wg.at[half(b, g), cols(sat, cw)]
        dst = wg.at[half(b, g), cols(p if s == 0 else sat, cw)]
        return rc(src, dst, wr.at[0, s, b, r], wr.at[1, s, b, r], dp=to)

    def y_w(b, r, s):
        k2 = lax.rem(k + nh - r, nh)
        h2 = hub_of(k2)
        at = wg.at[half(b, g), cols(h2 if s == 0 else 4 * k2 + 1 - h2, cw)]
        return rc(at, at, wy.at[0, s, b, r], wy.at[1, s, b, r], groups=1 - g)

    def y_sat(b):
        at = wg.at[half(b, g), cols(sat, cw)]
        return rc(at, at, wv.at[0, b], wv.at[1, b], groups=1 - g)

    def ret(b):
        return rc(obuf.at[:, cols(b, rb)], hg.at[:, cols(b, rb)],
                  out.at[0, b], out.at[1, b], dp=sat)

    def lr_copy(d):
        return rc(lrbuf.at[t], lrbuf.at[t], lrs.at[0, d], lrs.at[1, d],
                  tensor=lax.rem(t + d, T))

    def f_copy(d):
        return rc(featbuf.at[p], featbuf.at[p], fs_.at[0, d], fs_.at[1, d],
                  dp=lax.rem(p + d, n))

    bpt = n // T
    t_to, slot = p // bpt, lax.rem(p, bpt) * T + t

    def s_copy(d):
        p2 = lax.rem(p + d, n)
        return rc(sp.at[p2], spr.at[slot], sps.at[d], sprr.at[slot], dp=p2, tensor=t_to)

    def left_right():
        own_x.wait()
        left = lax.dot_general(hid[...], pin[...], NT, preferred_element_type=jnp.float32)
        right = lax.dot_general(xg[pl.ds(0, tok), cols(t, dcols)], pout[:, cols(t, dcols)], NT,
                                preferred_element_type=jnp.float32)
        lrbuf[t] = jnp.concatenate([left, right], axis=1)
        for d in range(1, T):
            lr_copy(d).start()

    def features():
        for d in range(1, T):
            lr_copy(d).wait_recv()
        R = featbuf.shape[1]
        row = lax.broadcasted_iota(jnp.int32, (R, 2 * kk), 0)
        lane = lax.broadcasted_iota(jnp.int32, (1, 2 * kk), 1)
        for e in range(ex):
            lr = lrbuf[0, pl.ds(e * SEQ, SEQ), :]
            for s in range(1, T):
                lr = lr + lrbuf[s, pl.ds(e * SEQ, SEQ), :]
            right = lr[:, kk:]
            gscr[e] = jnp.dot(lr.T, jnp.concatenate([right, right], axis=1),
                              precision=lax.Precision.HIGHEST,
                              preferred_element_type=jnp.float32)
        mine = [gscr[e, pl.ds(pl.multiple_of(t * srows, srows), srows), :] for e in range(ex)]
        for j in range(srows // 2):
            val = jnp.zeros((R, 2 * kk), jnp.float32)
            for e in range(ex):
                vec = jnp.where(lane < kk, mine[e][2 * j:2 * j + 1], mine[e][2 * j + 1:2 * j + 2])
                val = jnp.where(row == p * ex + e, vec, val)
            featbuf[p, :, pl.ds(j * 2 * kk, 2 * kk)] = val.astype(jnp.bfloat16)
        for d in range(1, n):
            f_copy(d).start()

    def partial_scores():
        for d in range(1, n):
            f_copy(d).wait_recv()
        every = featbuf[0].astype(jnp.float32)
        for s in range(1, n):
            every = every + featbuf[s].astype(jnp.float32)
        s = lax.dot_general(every.astype(jnp.bfloat16), q[...], NT, preferred_element_type=jnp.float32)
        sp[...] = jnp.zeros_like(sp)
        for i in range(n):
            sp[i, 0:ex, :] = s[i * ex:(i + 1) * ex]
        for d in range(1, n):
            s_copy(d).start()

        @pl.when(t_to == t)
        def _():
            spr[slot] = sp[p]

        @pl.when(t_to != t)
        def _():
            s_copy(0).start()

    def finish_scores():
        for i in range(bpt * T):
            me = jnp.logical_and(t * bpt + i // T == p, i % T == t)

            @pl.when(jnp.logical_not(me))
            def _():
                rc(sp.at[0], spr.at[i], sps.at[0], sprr.at[i], dp=p, tensor=t).wait_recv()

        for b in range(bpt):
            tot = spr[b * T, 0:ex, :]
            for s in range(1, T):
                tot = tot + spr[b * T + s, 0:ex, :]
            sc[:, pl.ds(b * nq, nq)] = tot

    @pl.when(p != hub)
    def _():
        order = [(b, 0) for b in range(VIA)]
        for b in range(VIA, NB):
            order.append((b, 0))
            if b > VIA:
                order.append((b - 1, 1))
        order.append((NB - 1, 1))
        sends = [sat_x(i) for i in range(XC)] + [sat_w(b, o) for b, o in order]
        for i, copy in enumerate(sends):
            if i >= WIN:
                sends[i - WIN].wait_send()
            copy.start()
            if i == WIN - 1:
                left_right()
            elif i == XC + 3:
                features()
            elif i == XC + 8:
                partial_scores()
        for copy in sends[-WIN:]:
            copy.wait_send()
        finish_scores()
        for b in range(NB):
            ret(b).wait_recv()

    @pl.when(p == hub)
    def _():
        for i in range(XC):
            for d in range(1, U):
                x_far(0, i, d).start()
            x_mate(0, i, 0).start()

        @pl.loop(0, NB)
        def _(b):
            @pl.loop(1, nh)
            def _(r):
                hub_w(b, r, 0).start()

        left_right()

        def pass_own(lo, hi):
            @pl.loop(lo, hi)
            def _(b):
                @pl.loop(1, nh)
                def _(r):
                    hub_w(b, r, 0).wait_recv()
                    y_w(b, r, 0).start()

        def pass_x(a, i):
            for d in range(1, U):
                x_far(a, i, d).wait_recv()
                x_mate(a, i, d).start()

        def take_sat(i):
            sat_x(i).wait_recv()
            for d in range(1, U):
                x_far(1, i, d).start()
            x_mate(1, i, 0).start()

        for i in range(XC):
            pass_own(NB * i // XC, NB * (i + 1) // XC)
            pass_x(0, i)
            take_sat(i)
        features()
        pass_x(1, 0)

        @pl.loop(0, NB + 2)
        def _(s):
            @pl.when(s < NB)
            def _():
                sat_w(s, 0).wait_recv()

                @pl.loop(1, nh)
                def _(r):
                    hub_w(s, r, 1).start()

                @pl.when(s < VIA)
                def _():
                    y_sat(s).start()

            @pl.when(jnp.logical_and(s >= 1, s <= NB))
            def _():
                @pl.loop(1, nh)
                def _(r):
                    hub_w(s - 1, r, 1).wait_recv()
                    y_w(s - 1, r, 1).start()

            @pl.when(s == 0)
            def _():
                for i in range(1, XC // 2):
                    pass_x(1, i)

            @pl.when(s == 1)
            def _():
                for i in range(XC // 2, XC):
                    pass_x(1, i)
                partial_scores()
                own_w.wait()
                for a in range(2):
                    for i in range(XC):
                        for d in range(U):
                            x_mate(a, i, d).wait_recv()

            @pl.when(s == 3)
            def _():
                finish_scores()

            @pl.when(s >= 2)
            def _():
                b = s - 2

                @pl.loop(1, nh)
                def _(r):
                    for j in range(2):
                        y_w(b, r, j).wait_recv()

                @pl.when(b < VIA)
                def _():
                    y_sat(b).wait_recv()

                @pl.when(b >= VIA)
                def _():
                    sat_w(b, 1).wait_recv()

                @pl.loop(0, tok // SEQ)
                def _(m):
                    at = pl.ds(pl.multiple_of(m * SEQ, SEQ), SEQ)
                    x = xg[pl.ds(pl.multiple_of(tok + m * SEQ, SEQ), SEQ), :]
                    obuf[at, cols(b, rb)] = lax.dot_general(
                        x, wg[blk(b), :], NT, preferred_element_type=jnp.float32
                    ).astype(jnp.bfloat16)

                ret(b).start()

                @pl.loop(0, tok // SEQ)
                def _(m):
                    at = pl.ds(pl.multiple_of(m * SEQ, SEQ), SEQ)
                    hg[at, cols(b, rb)] = lax.dot_general(
                        xg[at, :], wg[blk(b), :], NT, preferred_element_type=jnp.float32
                    ).astype(jnp.bfloat16)

        for a in range(2):
            for i in range(XC):
                for d in range(1, U):
                    x_far(a, i, d).wait_send()
                for d in range(U):
                    x_mate(a, i, d).wait_send()

        @pl.loop(0, NB)
        def _(b):
            @pl.loop(1, nh)
            def _(r):
                for s in range(2):
                    hub_w(b, r, s).wait_send()
                    y_w(b, r, s).wait_send()

            @pl.when(b < VIA)
            def _():
                y_sat(b).wait_send()

            ret(b).wait_send()

    for d in range(1, T):
        lr_copy(d).wait_send()
    for d in range(1, n):
        f_copy(d).wait_send()
        s_copy(d).wait_send()

    @pl.when(t_to != t)
    def _():
        s_copy(0).wait_send()


def local(n, T, hidden, out_grad, down_weight, proj_in, proj_out, queries):
    tok, dcols = out_grad.shape
    rows, cw = down_weight.shape
    kk = proj_in.shape[1]
    ex = tok // SEQ
    nq, fsz = queries.shape
    R = -(-n * ex // 16) * 16
    nh, U = n // 2, T // 2
    bf, f32 = jnp.bfloat16, jnp.float32
    vm, hb = pl.BlockSpec(memory_space=pltpu.VMEM), pl.BlockSpec(memory_space=pl.ANY)
    dma = pltpu.SemaphoreType.DMA
    return pl.pallas_call(
        functools.partial(kernel, n, T),
        out_shape=(jax.ShapeDtypeStruct((tok, rows), bf),
                   jax.ShapeDtypeStruct((ex, nq * n // T), f32)),
        in_specs=[vm, hb, hb, vm, vm, vm],
        out_specs=(vm, vm),
        scratch_shapes=[
            pltpu.VMEM((rows, cw * n), bf),
            pltpu.VMEM((2 * tok, dcols * T), bf),
            pltpu.VMEM((tok, rows), bf),
            pltpu.VMEM((T, tok, 2 * kk), f32),
            pltpu.VMEM((ex, 2 * kk, 2 * kk), f32),
            pltpu.VMEM((n, R, fsz), bf),
            pltpu.VMEM((n, 8, nq), f32),
            pltpu.VMEM((n // T * T, 8, nq), f32),
            dma((2,)),
            dma((2, XC)),
            dma((2, 2, XC, U)),
            dma((2, 2, XC, U)),
            dma((2, NB)),
            dma((2, NB)),
            dma((2, 2, NB, nh)),
            dma((2, 2, NB, nh)),
            dma((2, NB)),
            dma((2, NB)),
            dma((2, T)),
            dma((2, n)),
            dma((n,)),
            dma((n // T * T,)),
        ],
        compiler_params=pltpu.CompilerParams(
            collective_id=0, has_side_effects=True, vmem_limit_bytes=56 * 2**20),
        cost_estimate=pl.CostEstimate(flops=4 * tok * rows * cw * n, bytes_accessed=2 * rows * cw * n,
                                      transcendentals=0),
    )(hidden, out_grad, down_weight, proj_in.T, proj_out.T, queries)


def solution(mesh):
    in_specs = (
        P(("groups", "dp"), "tensor"),
        P(("groups", "dp"), "tensor"),
        P("tensor", "dp"),
        P("tensor", None),
        P(),
        P("dp", "tensor"),
    )
    out_specs = (P(("groups", "dp"), "tensor"), P(("groups", "dp"), "tensor"))
    body = functools.partial(local, mesh.shape["dp"], mesh.shape["tensor"])
    return jax.shard_map(body, mesh=mesh, in_specs=in_specs, out_specs=out_specs, check_vma=False)
```

```python
import functools

import jax
import jax.numpy as jnp
from jax import lax
from jax.experimental import pallas as pl
from jax.experimental.pallas import tpu as pltpu
from jax.sharding import PartitionSpec as P

SEQ = 256
NB = 7
VIA = 2
XC = 4
LAG = 3
WIN = 3
NT = (((1,), (1,)), ((), ()))


def kernel(n, T, hid_in, og, w, pin, pout, q_in, hg, sc,
           hid, q,
           wg, xg, obuf, lrbuf, gscr, featbuf, sp, spr,
           loc, xz, xo, xs, wsat, wsend, wr, wy, wv, out,
           lrs, fs_, sps, sprr):
    g, p, t = lax.axis_index("groups"), lax.axis_index("dp"), lax.axis_index("tensor")
    tok, dcols = og.shape
    rows, cw = w.shape
    rb = rows // NB
    hf = rb // 2
    xr = tok // XC
    ex = tok // SEQ
    kk = pin.shape[0]
    nh, U = n // 2, T // 2
    nq, fsz = q.shape
    srows = kk // T
    k = p // 2
    hub_of = lambda pair: 2 * pair + 1 - (4 * pair) // n
    hub = hub_of(k)
    sat = 4 * k + 1 - hub
    u, c = t // 2, lax.rem(t, 2)

    def rc(src, dst, ss, rs, **dev):
        return pltpu.make_async_remote_copy(
            src_ref=src, dst_ref=dst, send_sem=ss, recv_sem=rs,
            device_id=dev, device_id_type=pl.DeviceIdType.MESH)

    def cols(i, width):
        return pl.ds(pl.multiple_of(i * width, width), width)

    def half(b, h):
        return pl.ds(pl.multiple_of(b * rb + h * hf, hf), hf)

    def blk(b):
        return pl.ds(pl.multiple_of(b * rb, rb), rb)

    own_x = pltpu.make_async_copy(og, xg.at[pl.ds(0, tok), cols(t, dcols)], loc.at[0])
    own_w = pltpu.make_async_copy(w, wg.at[:, cols(p, cw)], loc.at[1])
    get_hid = pltpu.make_async_copy(hid_in, hid, loc.at[2])
    get_q = pltpu.make_async_copy(q_in, q, loc.at[3])
    own_x.start()
    get_hid.start()
    get_q.start()

    @pl.when(p == hub)
    def _():
        own_w.start()

    bar = pltpu.get_barrier_semaphore()

    @pl.loop(1, n * T)
    def _(i):
        other = lax.rem(p * T + t + i, n * T)
        pl.semaphore_signal(bar, inc=1, device_id={"dp": other // T, "tensor": lax.rem(other, T)},
                            device_id_type=pl.DeviceIdType.MESH)

    pl.semaphore_signal(bar, inc=1, device_id={"groups": 1 - g}, device_id_type=pl.DeviceIdType.MESH)
    pl.semaphore_wait(bar, n * T)

    def sat_x(i):
        return rc(og.at[pl.ds(i * xr, xr), :],
                  xg.at[pl.ds(tok + i * xr, xr), cols(t, dcols)],
                  xz.at[0, i], xz.at[1, i], dp=hub)

    def xrow(a, i):
        return pl.ds(a * tok + i * xr, xr)

    def x_far(a, i, d):
        u2 = lax.rem(u + d, U)
        src = og.at[pl.ds(i * xr, xr), :] if a == 0 else xg.at[xrow(a, i), cols(t, dcols)]
        return rc(src, xg.at[xrow(a, i), cols(t, dcols)],
                  xo.at[0, a, i, d], xo.at[1, a, i, d], tensor=2 * u2 + c)

    def x_mate(a, i, d):
        b = 2 * lax.rem(u + U - d, U) + c
        src = og.at[pl.ds(i * xr, xr), :] if a == 0 and d == 0 else xg.at[xrow(a, i), cols(b, dcols)]
        return rc(src, xg.at[xrow(a, i), cols(b, dcols)],
                  xs.at[0, a, i, d], xs.at[1, a, i, d], tensor=2 * u + 1 - c)

    def sat_w(b, o):
        h = g if o == 0 else 1 - g
        return rc(w.at[half(b, h), :], wg.at[half(b, h), cols(sat, cw)],
                  wsend.at[o, b], wsat.at[o, b], dp=hub)

    def hub_w(b, r, s):
        to = hub_of(lax.rem(k + r, nh))
        src = w.at[half(b, g), :] if s == 0 else wg.at[half(b, g), cols(sat, cw)]
        dst = wg.at[half(b, g), cols(p if s == 0 else sat, cw)]
        return rc(src, dst, wr.at[0, s, b, r], wr.at[1, s, b, r], dp=to)

    def y_w(b, r, s):
        k2 = lax.rem(k + nh - r, nh)
        h2 = hub_of(k2)
        at = wg.at[half(b, g), cols(h2 if s == 0 else 4 * k2 + 1 - h2, cw)]
        return rc(at, at, wy.at[0, s, b, r], wy.at[1, s, b, r], groups=1 - g)

    def y_sat(b):
        at = wg.at[half(b, g), cols(sat, cw)]
        return rc(at, at, wv.at[0, b], wv.at[1, b], groups=1 - g)

    def ret(b):
        return rc(obuf.at[:, cols(b, rb)], hg.at[:, cols(b, rb)],
                  out.at[0, b], out.at[1, b], dp=sat)

    def lr_copy(d):
        return rc(lrbuf.at[t], lrbuf.at[t], lrs.at[0, d], lrs.at[1, d],
                  tensor=lax.rem(t + d, T))

    def f_copy(d):
        return rc(featbuf.at[p], featbuf.at[p], fs_.at[0, d], fs_.at[1, d],
                  dp=lax.rem(p + d, n))

    bpt = n // T
    t_to, slot = p // bpt, lax.rem(p, bpt) * T + t

    def s_copy(d):
        p2 = lax.rem(p + d, n)
        return rc(sp.at[p2], spr.at[slot], sps.at[d], sprr.at[slot], dp=p2, tensor=t_to)

    def left_right():
        own_x.wait()
        get_hid.wait()
        left = lax.dot_general(hid[...], pin[...], NT, preferred_element_type=jnp.float32)
        right = lax.dot_general(xg[pl.ds(0, tok), cols(t, dcols)], pout[:, cols(t, dcols)], NT,
                                preferred_element_type=jnp.float32)
        lrbuf[t] = jnp.concatenate([left, right], axis=1)
        for d in range(1, T):
            lr_copy(d).start()

    def features():
        for d in range(1, T):
            lr_copy(d).wait_recv()
        R = featbuf.shape[1]
        row = lax.broadcasted_iota(jnp.int32, (R, 2 * kk), 0)
        lane = lax.broadcasted_iota(jnp.int32, (1, 2 * kk), 1)
        for e in range(ex):
            lr = lrbuf[0, pl.ds(e * SEQ, SEQ), :]
            for s in range(1, T):
                lr = lr + lrbuf[s, pl.ds(e * SEQ, SEQ), :]
            right = lr[:, kk:]
            gscr[e] = jnp.dot(lr.T, jnp.concatenate([right, right], axis=1),
                              precision=lax.Precision.HIGHEST,
                              preferred_element_type=jnp.float32)
        mine = [gscr[e, pl.ds(pl.multiple_of(t * srows, srows), srows), :] for e in range(ex)]
        for j in range(srows // 2):
            val = jnp.zeros((R, 2 * kk), jnp.float32)
            for e in range(ex):
                vec = jnp.where(lane < kk, mine[e][2 * j:2 * j + 1], mine[e][2 * j + 1:2 * j + 2])
                val = jnp.where(row == p * ex + e, vec, val)
            featbuf[p, :, pl.ds(j * 2 * kk, 2 * kk)] = val.astype(jnp.bfloat16)
        for d in range(1, n):
            f_copy(d).start()

    def partial_scores():
        get_q.wait()
        for d in range(1, n):
            f_copy(d).wait_recv()
        every = featbuf[0].astype(jnp.float32)
        for s in range(1, n):
            every = every + featbuf[s].astype(jnp.float32)
        s = lax.dot_general(every.astype(jnp.bfloat16), q[...], NT, preferred_element_type=jnp.float32)
        sp[...] = jnp.zeros_like(sp)
        for i in range(n):
            sp[i, 0:ex, :] = s[i * ex:(i + 1) * ex]
        for d in range(1, n):
            s_copy(d).start()

        @pl.when(t_to == t)
        def _():
            spr[slot] = sp[p]

        @pl.when(t_to != t)
        def _():
            s_copy(0).start()

    def finish_scores():
        for i in range(bpt * T):
            me = jnp.logical_and(t * bpt + i // T == p, i % T == t)

            @pl.when(jnp.logical_not(me))
            def _():
                rc(sp.at[0], spr.at[i], sps.at[0], sprr.at[i], dp=p, tensor=t).wait_recv()

        for b in range(bpt):
            tot = spr[b * T, 0:ex, :]
            for s in range(1, T):
                tot = tot + spr[b * T + s, 0:ex, :]
            sc[:, pl.ds(b * nq, nq)] = tot

    @pl.when(p != hub)
    def _():
        order = [(b, 0) for b in range(VIA)]
        for b in range(VIA, NB):
            order.append((b, 0))
            if b > VIA:
                order.append((b - 1, 1))
        order.append((NB - 1, 1))
        sends = [sat_x(i) for i in range(XC)] + [sat_w(b, o) for b, o in order]
        for i, copy in enumerate(sends):
            if i >= WIN:
                sends[i - WIN].wait_send()
            copy.start()
            if i == WIN - 1:
                left_right()
            elif i == XC + 3:
                features()
        for copy in sends[-WIN:]:
            copy.wait_send()
        partial_scores()
        finish_scores()
        for b in range(NB):
            ret(b).wait_recv()

    @pl.when(p == hub)
    def _():
        for i in range(XC):
            for d in range(1, U):
                x_far(0, i, d).start()
            x_mate(0, i, 0).start()

        @pl.loop(0, NB)
        def _(b):
            @pl.loop(1, nh)
            def _(r):
                hub_w(b, r, 0).start()

        def pass_own(lo, hi):
            @pl.loop(lo, hi)
            def _(b):
                @pl.loop(1, nh)
                def _(r):
                    hub_w(b, r, 0).wait_recv()
                    y_w(b, r, 0).start()

        def pass_x(a, i):
            for d in range(1, U):
                x_far(a, i, d).wait_recv()
                x_mate(a, i, d).start()

        def take_sat(i):
            sat_x(i).wait_recv()
            for d in range(1, U):
                x_far(1, i, d).start()
            x_mate(1, i, 0).start()

        for i in range(XC):
            pass_own(NB * i // XC, NB * (i + 1) // XC)
            pass_x(0, i)
            take_sat(i)
        left_right()

        @pl.loop(0, NB + LAG)
        def _(s):
            @pl.when(s < NB)
            def _():
                sat_w(s, 0).wait_recv()

                @pl.loop(1, nh)
                def _(r):
                    hub_w(s, r, 1).start()

                @pl.when(s < VIA)
                def _():
                    y_sat(s).start()

            @pl.when(jnp.logical_and(s >= 1, s <= NB))
            def _():
                @pl.loop(1, nh)
                def _(r):
                    hub_w(s - 1, r, 1).wait_recv()
                    y_w(s - 1, r, 1).start()

            for i in range(XC):
                @pl.when(s == i)
                def _():
                    pass_x(1, i)

            @pl.when(s == LAG)
            def _():
                own_w.wait()
                for a in range(2):
                    for i in range(XC):
                        for d in range(U):
                            x_mate(a, i, d).wait_recv()

            @pl.when(s >= LAG)
            def _():
                b = s - LAG

                @pl.loop(1, nh)
                def _(r):
                    for j in range(2):
                        y_w(b, r, j).wait_recv()

                @pl.when(b < VIA)
                def _():
                    y_sat(b).wait_recv()

                @pl.when(b >= VIA)
                def _():
                    sat_w(b, 1).wait_recv()

                @pl.loop(0, tok // SEQ)
                def _(m):
                    at = pl.ds(pl.multiple_of(m * SEQ, SEQ), SEQ)
                    x = xg[pl.ds(pl.multiple_of(tok + m * SEQ, SEQ), SEQ), :]
                    obuf[at, cols(b, rb)] = lax.dot_general(
                        x, wg[blk(b), :], NT, preferred_element_type=jnp.float32
                    ).astype(jnp.bfloat16)

                ret(b).start()

                @pl.loop(0, tok // SEQ)
                def _(m):
                    at = pl.ds(pl.multiple_of(m * SEQ, SEQ), SEQ)
                    hg[at, cols(b, rb)] = lax.dot_general(
                        xg[at, :], wg[blk(b), :], NT, preferred_element_type=jnp.float32
                    ).astype(jnp.bfloat16)

            @pl.when(s == LAG + 1)
            def _():
                features()

            @pl.when(s == NB - 1)
            def _():
                partial_scores()

        finish_scores()

        for a in range(2):
            for i in range(XC):
                for d in range(1, U):
                    x_far(a, i, d).wait_send()
                for d in range(U):
                    x_mate(a, i, d).wait_send()

        @pl.loop(0, NB)
        def _(b):
            @pl.loop(1, nh)
            def _(r):
                for s in range(2):
                    hub_w(b, r, s).wait_send()
                    y_w(b, r, s).wait_send()

            @pl.when(b < VIA)
            def _():
                y_sat(b).wait_send()

            ret(b).wait_send()

    for d in range(1, T):
        lr_copy(d).wait_send()
    for d in range(1, n):
        f_copy(d).wait_send()
        s_copy(d).wait_send()

    @pl.when(t_to != t)
    def _():
        s_copy(0).wait_send()


def local(n, T, hidden, out_grad, down_weight, proj_in, proj_out, queries):
    tok, dcols = out_grad.shape
    rows, cw = down_weight.shape
    kk = proj_in.shape[1]
    ex = tok // SEQ
    nq, fsz = queries.shape
    R = -(-n * ex // 16) * 16
    nh, U = n // 2, T // 2
    bf, f32 = jnp.bfloat16, jnp.float32
    vm, hb = pl.BlockSpec(memory_space=pltpu.VMEM), pl.BlockSpec(memory_space=pl.ANY)
    dma = pltpu.SemaphoreType.DMA
    return pl.pallas_call(
        functools.partial(kernel, n, T),
        out_shape=(jax.ShapeDtypeStruct((tok, rows), bf),
                   jax.ShapeDtypeStruct((ex, nq * n // T), f32)),
        in_specs=[hb, hb, hb, vm, vm, hb],
        out_specs=(vm, vm),
        scratch_shapes=[
            pltpu.VMEM(hidden.shape, bf),
            pltpu.VMEM(queries.shape, bf),
            pltpu.VMEM((rows, cw * n), bf),
            pltpu.VMEM((2 * tok, dcols * T), bf),
            pltpu.VMEM((tok, rows), bf),
            pltpu.VMEM((T, tok, 2 * kk), f32),
            pltpu.VMEM((ex, 2 * kk, 2 * kk), f32),
            pltpu.VMEM((n, R, fsz), bf),
            pltpu.VMEM((n, 8, nq), f32),
            pltpu.VMEM((n // T * T, 8, nq), f32),
            dma((4,)),
            dma((2, XC)),
            dma((2, 2, XC, U)),
            dma((2, 2, XC, U)),
            dma((2, NB)),
            dma((2, NB)),
            dma((2, 2, NB, nh)),
            dma((2, 2, NB, nh)),
            dma((2, NB)),
            dma((2, NB)),
            dma((2, T)),
            dma((2, n)),
            dma((n,)),
            dma((n // T * T,)),
        ],
        compiler_params=pltpu.CompilerParams(
            collective_id=0, has_side_effects=True, vmem_limit_bytes=56 * 2**20),
        cost_estimate=pl.CostEstimate(flops=4 * tok * rows * cw * n, bytes_accessed=2 * rows * cw * n,
                                      transcendentals=0),
    )(hidden, out_grad, down_weight, proj_in.T, proj_out.T, queries)


def solution(mesh):
    in_specs = (
        P(("groups", "dp"), "tensor"),
        P(("groups", "dp"), "tensor"),
        P("tensor", "dp"),
        P("tensor", None),
        P(),
        P("dp", "tensor"),
    )
    out_specs = (P(("groups", "dp"), "tensor"), P(("groups", "dp"), "tensor"))
    body = functools.partial(local, mesh.shape["dp"], mesh.shape["tensor"])
    return jax.shard_map(body, mesh=mesh, in_specs=in_specs, out_specs=out_specs, check_vma=False)
```
